256 devices in a mesh: tile: 64 (over y, x_hi, z), day: 4 (over x_lo, core).
Axes of the slice: x: 4 (x_hi: 2, x_lo: 2; x = x_hi * 2 + x_lo), y: 4, z: 8, core: 2. Of those that a mesh axis runs over, the one named last changes fastest.
Arguments:
- source_spectra: bfloat16 [16, 64, 2, 1024], P('day', 'tile'), may hold values from -6 to 6
- receiver_spectra: bfloat16 [16, 1024, 2, 1024], P('day', 'tile'), may hold values from -6 to 6
- valid_pairs: int32 [16, 64, 1024], P('day', None, 'tile'), may hold values 0 or 1
Outputs:
- mean_day_stack: float32 [64, 1024, 401], P(None, 'tile')
- phase_weighted: float32 [64, 1024, 401], P(None, 'tile')
The draws below stay inside these ranges and needn't reach their ends.
All inputs are finite; a program needn't handle non-finite values. No bound on the sum of `valid_pairs` on one device may be relied on, other than what follows from the above.
Results may differ from the reference program's by a relative error of at most 0.0055.
Values may be sent and summed in bfloat16 or wider, within the bound.
No kernel may reach another device: no remote copies, remote signals or barrier semaphores. Data moves between devices by JAX's collectives and lax.ppermute only.
A program may use at most 128 MiB of HBM per device.

```python
import math
import jax
import jax.numpy as jnp
from jax import lax

F = 1024
MAXLAG = 200
S = 64
R = 1024
DAYS = 16


def plant(values, stream_key, smallest, high):
    spot = [jax.random.randint(jax.random.fold_in(stream_key, axis), (), 0, length) for axis, length in enumerate(values.shape)]
    widest = values.shape.index(max(values.shape))
    next_to = spot[:widest] + [(spot[widest] + 1) % values.shape[widest]] + spot[widest + 1:]
    return values.at[tuple(spot)].set(smallest).at[tuple(next_to)].set(high)


def block_levels(rng, dims, shards, low, largest):
    def one(position, parts):
        heights = jax.random.uniform(jax.random.fold_in(jax.random.fold_in(rng, 6), position), (parts,), jnp.float32, low / len(shards), largest / len(shards))
        return jnp.repeat(jnp.exp(heights), dims[position] // parts).reshape((-1,) + (1,) * (len(dims) - position - 1))

    gain = one(*shards[0])
    for cut in shards[1:]:
        gain = gain * one(*cut)
    return gain


def bell_draw(key, shape, scale, most, shards=(), kind=jnp.bfloat16):
    result = scale * jax.random.normal(key, shape, jnp.float32)
    if shards:
        result = result * block_levels(key, shape, shards, -0.22, 0.18)
    return jnp.clip(result, -most, most).astype(kind)


def setup_inputs(seed: int = 0) -> dict:
    arg_keys = jax.random.split(jax.random.key(seed), 4)
    return {
        "source_spectra": bell_draw(arg_keys[0], (DAYS, S, 2, F), 1.0, 6.0, ((0, 4), (1, 64))),
        "receiver_spectra": bell_draw(arg_keys[1], (DAYS, R, 2, F), 1.0, 6.0, ((0, 4), (1, 64))),
        "valid_pairs": plant((jax.random.randint(arg_keys[2], (DAYS, S, R), 0, 2) < 1).astype(jnp.int32), jax.random.fold_in(arg_keys[2], 1), 0, 1),
    }


def lag_basis_table(frequency_count, max_lag):
    samples = 2 * frequency_count
    freq_index = jnp.arange(frequency_count, dtype=jnp.int32)
    lag_index = jnp.arange(2 * max_lag + 1, dtype=jnp.int32) - max_lag
    phase_turns = jnp.mod(freq_index[:, None] * lag_index[None, :], samples).astype(jnp.float32)
    angles = phase_turns * (2.0 * math.pi / samples)
    weight = jnp.where(freq_index == 0, 0.5, 1.0).astype(jnp.float32)[:, None] * frequency_count ** (-0.5)
    cosine = weight * jnp.cos(angles)
    sine = weight * jnp.sin(angles)
    upper_half = jnp.concatenate([cosine, sine], axis=1)
    negative_lag_half = jnp.concatenate([-sine, cosine], axis=1)
    return jnp.concatenate([upper_half, negative_lag_half], axis=0).astype(jnp.bfloat16)

def one_source(source_days, receiver_spectra, weights, lag_fourier_matrix):
    source_real = source_days[:, 0].astype(jnp.float32)[:, None, :]
    source_imag = source_days[:, 1].astype(jnp.float32)[:, None, :]
    receiver_real = receiver_spectra[:, :, 0].astype(jnp.float32)
    receiver_imag = receiver_spectra[:, :, 1].astype(jnp.float32)
    cross_real = source_real * receiver_real + source_imag * receiver_imag
    cross_imag = source_real * receiver_imag - source_imag * receiver_real
    cross_spectrum = jnp.concatenate([cross_real, cross_imag], axis=-1).astype(jnp.bfloat16)
    analytic_signal = jnp.einsum('tsc,cz->tsz', cross_spectrum.astype(jnp.float32), lag_fourier_matrix.astype(jnp.float32))
    lag_count = lag_fourier_matrix.shape[1] // 2
    real_part = analytic_signal[..., :lag_count]
    imag_part = analytic_signal[..., lag_count:]
    inverse_norm = lax.rsqrt(real_part * real_part + imag_part * imag_part + 0.0625)
    mask_lags = weights[:, :, None]
    linear = lax.optimization_barrier(jnp.sum(mask_lags * real_part, axis=0))
    phase_real = lax.optimization_barrier(jnp.sum(mask_lags * real_part * inverse_norm, axis=0))
    phase_imag = lax.optimization_barrier(jnp.sum(mask_lags * imag_part * inverse_norm, axis=0))
    return jnp.stack([linear, phase_real, phase_imag], axis=0)

def reference(source_spectra, receiver_spectra, valid_pairs):
    lag_fourier_matrix = lag_basis_table(F, MAXLAG)
    weights_all = valid_pairs.astype(jnp.float32)

    def per_source(items):
        source_days, weights = items
        return one_source(source_days, receiver_spectra, weights, lag_fourier_matrix)
    running_totals = lax.map(per_source, (jnp.moveaxis(source_spectra, 1, 0), jnp.moveaxis(weights_all, 1, 0)))
    counts = lax.optimization_barrier(jnp.sum(weights_all, axis=0))
    divisor = jnp.maximum(counts, 1.0)[:, :, None]
    mean_day_stack = running_totals[:, 0] / divisor
    coherence = (running_totals[:, 1] * running_totals[:, 1] + running_totals[:, 2] * running_totals[:, 2]) / (divisor * divisor)
    return (mean_day_stack, mean_day_stack * coherence)
```

```python
import math

import jax
import jax.numpy as jnp
import numpy as np
from jax import lax
from jax.experimental import pallas as pl
from jax.experimental.pallas import tpu as pltpu
from jax.sharding import PartitionSpec as P

MAXLAG = 200
HALF = 256
TILES, DAYS = 64, 4
PER = 4


def half_basis(frequency_count):
    samples = 2 * frequency_count
    freq = np.arange(frequency_count)[:, None]
    lag = np.arange(MAXLAG + 1)[None, :]
    angles = ((freq * lag) % samples) * (2.0 * math.pi / samples)
    weight = np.where(freq == 0, 0.5, 1.0) * frequency_count ** (-0.5)
    table = np.zeros((frequency_count, 2 * HALF))
    table[:, : MAXLAG + 1] = weight * np.cos(angles)
    table[:, HALF : HALF + MAXLAG + 1] = weight * np.sin(angles)
    return jnp.asarray(table, jnp.bfloat16)


def lag_order():
    table = np.zeros((2 * HALF, 2 * HALF))
    lag = np.arange(MAXLAG + 1)
    table[lag, MAXLAG + lag] = 1.0
    table[HALF + lag[1:], MAXLAG - lag[1:]] = 1.0
    return jnp.asarray(table, jnp.bfloat16)


def stack_kernel(shift_ref, src_ref, rec0, rec1, rec2, rec3, mask_ref, basis_ref, out_ref,
                 rec_f32, src_f32, lhs_r, lhs_i, res_r, res_i, done):
    shift = shift_ref[0]
    for j, rec in enumerate((rec0, rec1, rec2, rec3)):
        rec_f32[pl.ds((j ^ shift) * PER, PER)] = rec[...].astype(jnp.float32)
    for s in range(PER):
        src_f32[s] = src_ref[s].astype(jnp.float32)
    width = basis_ref.shape[0]
    for s in range(PER):
        p = s % 2
        for d in range(4 * PER):
            rows = slice(d * 16, d * 16 + 16)
            for lane in range(0, width, 256):
                cols = slice(lane, lane + 256)
                a = src_f32[s, 2 * d : 2 * d + 1, cols]
                b = src_f32[s, 2 * d + 1 : 2 * d + 2, cols]
                c = rec_f32[d, 0, :, cols]
                e = rec_f32[d, 1, :, cols]
                lhs_r[p, rows, cols] = (a * c + b * e).astype(jnp.bfloat16)
                lhs_i[p, rows, cols] = (a * e - b * c).astype(jnp.bfloat16)
        res_r[p] = jnp.dot(lhs_r[p], basis_ref[...], preferred_element_type=jnp.float32)
        res_i[p] = jnp.dot(lhs_i[p], basis_ref[...], preferred_element_type=jnp.float32)
        for h in range(0, 16, 8):
            zero = jnp.zeros((8, 128), jnp.float32)
            sums = [[zero] * 6 for _ in range(2)]
            count = zero
            for d in range(4 * PER):
                rows = slice(d * 16 + h, d * 16 + h + 8)
                col = s * 4 * PER + d
                m = jnp.broadcast_to(mask_ref[h : h + 8, col : col + 1], (8, 128))
                count = count + m
                for i in range(2):
                    lo = slice(i * 128, i * 128 + 128)
                    hi = slice(HALF + i * 128, HALF + i * 128 + 128)
                    rc, rs = res_r[p, rows, lo], res_r[p, rows, hi]
                    ic, is_ = res_i[p, rows, lo], res_i[p, rows, hi]
                    for sign, (u, v) in enumerate(((rc - is_, ic + rs), (rc + is_, ic - rs))):
                        w = m * lax.rsqrt(u * u + v * v + 0.0625)
                        acc = sums[i]
                        acc[3 * sign] = acc[3 * sign] + m * u
                        acc[3 * sign + 1] = acc[3 * sign + 1] + w * u
                        acc[3 * sign + 2] = acc[3 * sign + 2] + w * v
            inverse = 1.0 / jnp.maximum(count, 1.0)
            for i in range(2):
                for sign in range(2):
                    linear, real, imag = sums[i][3 * sign : 3 * sign + 3]
                    mean = linear * inverse
                    cols = slice(sign * HALF + i * 128, sign * HALF + i * 128 + 128)
                    done[0, h : h + 8, cols] = mean
                    done[1, h : h + 8, cols] = mean * ((real * real + imag * imag) * (inverse * inverse))
        out_ref[0, s] = done[0].astype(jnp.bfloat16)
        out_ref[1, s] = done[1].astype(jnp.bfloat16)


def stack_group(shift, sources, receivers, mask, basis):
    width = sources.shape[-1]
    whole = pl.BlockSpec(memory_space=pltpu.VMEM)
    rows = 4 * PER * 16
    return pl.pallas_call(
        stack_kernel,
        out_shape=jax.ShapeDtypeStruct((2, PER, 16, 2 * HALF), jnp.bfloat16),
        in_specs=[pl.BlockSpec(memory_space=pltpu.SMEM)] + [whole] * 7,
        out_specs=whole,
        scratch_shapes=[
            pltpu.VMEM((4 * PER, 2, 16, width), jnp.float32),
            pltpu.VMEM((PER, 8 * PER, width), jnp.float32),
            pltpu.VMEM((2, rows, width), jnp.bfloat16),
            pltpu.VMEM((2, rows, width), jnp.bfloat16),
            pltpu.VMEM((2, rows, 2 * HALF), jnp.float32),
            pltpu.VMEM((2, rows, 2 * HALF), jnp.float32),
            pltpu.VMEM((2, 16, 2 * HALF), jnp.float32),
        ],
        compiler_params=pltpu.CompilerParams(vmem_limit_bytes=32 * 2**20),
        cost_estimate=pl.CostEstimate(
            flops=2 * 2 * PER * rows * width * 2 * HALF, bytes_accessed=3 * 2**20, transcendentals=0
        ),
        name="stack_group",
    )(shift, sources, *receivers, mask, basis)


def order_kernel(where_ref, order_ref, *refs):
    parts, (mean_ref, weighted_ref) = refs[:16], refs[16:]
    y, xh, z0, day = (where_ref[i] for i in range(4))
    for k3 in range(4):
        for j in range(4):
            part = parts[4 * k3 + j][...].reshape(2 * PER * 16, 2 * HALF)
            full = jnp.dot(part, order_ref[...], preferred_element_type=jnp.float32)
            for k2 in range(PER):
                source = ((y ^ k3) << 4) | ((xh ^ (k2 >> 1)) << 3) | ((day ^ j) << 1) | (z0 ^ (k2 & 1))
                mean_ref[source] = full[k2 * 16 : k2 * 16 + 16, : 2 * MAXLAG + 1]
                low = (PER + k2) * 16
                weighted_ref[source] = full[low : low + 16, : 2 * MAXLAG + 1]


def order_outputs(where, parts):
    whole = pl.BlockSpec(memory_space=pltpu.VMEM)
    shape = jax.ShapeDtypeStruct((TILES, 16, 2 * MAXLAG + 1), jnp.float32)
    return pl.pallas_call(
        order_kernel,
        out_shape=(shape, shape),
        in_specs=[pl.BlockSpec(memory_space=pltpu.SMEM)] + [whole] * 17,
        out_specs=(whole, whole),
        compiler_params=pltpu.CompilerParams(vmem_limit_bytes=32 * 2**20),
        name="order_outputs",
    )(where, lag_order(), *parts)


def flip_bits(x, axis, amount, bits):
    shape = x.shape
    for bit in range(bits):
        step = 1 << bit
        view = x.reshape(shape[:axis] + (shape[axis] // (2 * step), 2, step) + shape[axis + 1 :])
        view = jnp.where((amount >> bit) & 1 == 1, jnp.flip(view, axis + 1), view)
        x = view.reshape(shape)
    return x


def day_swap(x, k):
    return lax.ppermute(x, "day", [(i, i ^ k) for i in range(DAYS)])


def tile_swap(x, k):
    return lax.ppermute(x, "tile", [(i, i ^ k) for i in range(TILES)])


def turn(x, k):
    pairs = []
    for t in range(TILES):
        for d in range(DAYS):
            to = (t & ~6) | ((d ^ k) << 1)
            pairs.append((t * DAYS + d, to * DAYS + ((t >> 1) & 3)))
    return lax.ppermute(x, ("tile", "day"), pairs)


def on_device(source_spectra, receiver_spectra, valid_pairs):
    width = source_spectra.shape[3]
    tile, day = lax.axis_index("tile"), lax.axis_index("day")
    y, xh, low, z0 = tile >> 4, (tile >> 3) & 1, (tile >> 1) & 3, tile & 1
    shift = low ^ day

    own = source_spectra.reshape(8, width)
    first = jnp.concatenate([turn(own, k) for k in range(4)], axis=0)

    rec0 = jnp.transpose(receiver_spectra, (0, 2, 1, 3))
    rec2 = day_swap(rec0, 2)
    rec1 = day_swap(rec0, 1)
    rec3 = day_swap(rec2, 1)

    m0 = valid_pairs.astype(jnp.bfloat16).reshape(32, 128)
    m2 = day_swap(m0, 2)
    m1 = day_swap(m0, 1)
    m3 = day_swap(m2, 1)
    masks = jnp.stack([m0, m1, m2, m3]).reshape(4, 4, 4, 2, 4, 2, 16)
    masks = lax.dynamic_index_in_dim(masks, day, axis=4, keepdims=False)
    masks = flip_bits(masks, 0, shift, 2)
    masks = flip_bits(masks, 2, y, 2)
    masks = flip_bits(masks, 3, xh, 1)
    masks = flip_bits(masks, 4, z0, 1)
    masks = jnp.transpose(masks, (2, 5, 3, 4, 0, 1)).reshape(4, 16, 64).astype(jnp.float32)
    masks = jnp.pad(masks, ((0, 0), (0, 0), (0, 64)))

    second = jnp.stack([first] + [tile_swap(first, k) for k in (1, 8, 9)])
    groups = [second] + [tile_swap(second, 16 * k) for k in (1, 2, 3)]

    basis = half_basis(width)
    shift_arg = shift.reshape(1).astype(jnp.int32)
    parts = []
    for k3 in range(4):
        mine = stack_group(shift_arg, groups[k3], (rec0, rec1, rec2, rec3), masks[k3], basis)
        across = day_swap(mine, 2)
        parts += [mine, day_swap(mine, 1), across, day_swap(across, 1)]
    where = jnp.stack([y, xh, z0, day]).astype(jnp.int32)
    return order_outputs(where, parts)


def solution(mesh):
    in_specs = (P("day", "tile", None, None), P("day", "tile", None, None), P("day", None, "tile"))
    out_specs = (P(None, "tile", None), P(None, "tile", None))
    return jax.shard_map(
        on_device, mesh=mesh, in_specs=in_specs, out_specs=out_specs, check_vma=False
    )
```

```python
import math

import jax
import jax.numpy as jnp
import numpy as np
from jax import lax
from jax.experimental import pallas as pl
from jax.experimental.pallas import tpu as pltpu
from jax.sharding import PartitionSpec as P

MAXLAG = 200
HALF = 256
TILES, DAYS = 64, 4

PER = 4


def half_basis(frequency_count):
    samples = 2 * frequency_count
    freq = np.arange(frequency_count)[:, None]
    lag = np.arange(MAXLAG + 1)[None, :]
    angles = ((freq * lag) % samples) * (2.0 * math.pi / samples)
    weight = np.where(freq == 0, 0.5, 1.0) * frequency_count ** (-0.5)
    table = np.zeros((frequency_count, 2 * HALF))
    table[:, : MAXLAG + 1] = weight * np.cos(angles)
    table[:, HALF : HALF + MAXLAG + 1] = weight * np.sin(angles)
    return jnp.asarray(table, jnp.bfloat16)


def lag_order():
    table = np.zeros((2 * HALF, 2 * HALF))
    lag = np.arange(MAXLAG + 1)
    table[lag, MAXLAG + lag] = 1.0
    table[HALF + lag[1:], MAXLAG - lag[1:]] = 1.0
    return jnp.asarray(table, jnp.bfloat16)


def widen_kernel(where_ref, rec0, rec1, rec2, rec3, out_ref, mask_ref, rows_ref):
    y, middle, day, shift = (where_ref[i] for i in range(4))
    width = out_ref.shape[-1]
    for j, rec in enumerate((rec0, rec1, rec2, rec3)):
        k = j ^ shift
        wide = rec[: 32 * PER].astype(jnp.float32)
        out_ref[pl.ds(k * PER, PER)] = wide.reshape(PER, 2, 16, width)
        rows_ref[k] = rec[32 * PER :]
    rows = rows_ref[...].reshape(64, width)
    gap = lax.broadcasted_iota(jnp.int32, (16, width), 1) - lax.broadcasted_iota(jnp.int32, (16, width), 0)
    for k3 in range(4):
        picks = []
        for k2 in range(PER):
            source = source_index(y ^ k3, day, middle ^ k2)
            picks.append(jnp.where(gap == source * 16, 1.0, 0.0).astype(jnp.bfloat16))
        chosen = lax.dot_general(
            jnp.concatenate(picks, axis=0), rows, (((1,), (1,)), ((), ())),
            preferred_element_type=jnp.float32,
        )
        mask_ref[k3, :, :, :64] = chosen.reshape(PER, 16, 64)


def source_index(y, day, middle):
    return (y << 4) | ((day >> 1) << 3) | (middle << 1) | (day & 1)


def widen_receivers(where, receivers):
    whole = pl.BlockSpec(memory_space=pltpu.VMEM)
    width = receivers[0].shape[-1]
    return pl.pallas_call(
        widen_kernel,
        out_shape=(
            jax.ShapeDtypeStruct((4 * PER, 2, 16, width), jnp.float32),
            jax.ShapeDtypeStruct((4, PER, 16, 128), jnp.float32),
        ),
        in_specs=[pl.BlockSpec(memory_space=pltpu.SMEM)] + [whole] * 4,
        out_specs=(whole, whole),
        scratch_shapes=[pltpu.VMEM((4, 16, width), jnp.bfloat16)],
        compiler_params=pltpu.CompilerParams(vmem_limit_bytes=16 * 2**20),
        name="widen_receivers",
    )(where, *receivers)


def stack_kernel(src_ref, rec_ref, mask_ref, basis_ref, *refs):
    out_ref, src_f32, lhs, res, done = refs[-5:]
    days, half = 4 * PER, lhs.shape[1] // 2
    width = basis_ref.shape[0]
    src_f32[...] = src_ref[...].astype(jnp.float32)
    for s in range(PER):
        p = s % 2
        for d in range(days):
            rows = slice(d * 16, d * 16 + 16)
            low = slice(half + d * 16, half + d * 16 + 16)
            row = (d // PER * PER + s) * 2 * PER + d % PER * 2
            for lane in range(0, width, 256):
                cols = slice(lane, lane + 256)
                a = src_f32[row : row + 1, cols]
                b = src_f32[row + 1 : row + 2, cols]
                c = rec_ref[d, 0, :, cols]
                e = rec_ref[d, 1, :, cols]
                lhs[p, rows, cols] = (a * c + b * e).astype(jnp.bfloat16)
                lhs[p, low, cols] = (a * e - b * c).astype(jnp.bfloat16)
        res[p] = jnp.dot(lhs[p], basis_ref[...], preferred_element_type=jnp.float32)
        for h in range(0, 16, 8):
            zero = jnp.zeros((8, 128), jnp.float32)
            sums = [[zero] * 6 for _ in range(2)]
            count = zero
            for d in range(days):
                rows = slice(d * 16 + h, d * 16 + h + 8)
                low = slice(half + d * 16 + h, half + d * 16 + h + 8)
                col = (d // PER) * 16 + d % PER
                m = jnp.broadcast_to(mask_ref[s, h : h + 8, col : col + 1], (8, 128))
                count = count + m
                for i in range(2):
                    cos = slice(i * 128, i * 128 + 128)
                    sin = slice(HALF + i * 128, HALF + i * 128 + 128)
                    rc, rs = res[p, rows, cos], res[p, rows, sin]
                    ic, is_ = res[p, low, cos], res[p, low, sin]
                    for sign, (u, v) in enumerate(((rc - is_, ic + rs), (rc + is_, ic - rs))):
                        w = m * lax.rsqrt(u * u + v * v + 0.0625)
                        acc = sums[i]
                        acc[3 * sign] = acc[3 * sign] + m * u
                        acc[3 * sign + 1] = acc[3 * sign + 1] + w * u
                        acc[3 * sign + 2] = acc[3 * sign + 2] + w * v
            inverse = 1.0 / jnp.maximum(count, 1.0)
            for i in range(2):
                for sign in range(2):
                    linear, real, imag = sums[i][3 * sign : 3 * sign + 3]
                    mean = linear * inverse
                    cols = slice(sign * HALF + i * 128, sign * HALF + i * 128 + 128)
                    done[0, h : h + 8, cols] = mean
                    done[1, h : h + 8, cols] = mean * ((real * real + imag * imag) * (inverse * inverse))
        out_ref[0, s] = done[0].astype(jnp.bfloat16)
        out_ref[1, s] = done[1].astype(jnp.bfloat16)


def stack_group(sources, receivers, mask, basis, earlier):
    width = sources.shape[-1]
    whole = pl.BlockSpec(memory_space=pltpu.VMEM)
    rows = 2 * 4 * PER * 16
    return pl.pallas_call(
        stack_kernel,
        out_shape=jax.ShapeDtypeStruct((2, PER, 16, 2 * HALF), jnp.bfloat16),
        in_specs=[whole] * 4 + [pl.BlockSpec(memory_space=pl.ANY)] * len(earlier),
        out_specs=whole,
        scratch_shapes=[
            pltpu.VMEM(sources.shape, jnp.float32),
            pltpu.VMEM((2, rows, width), jnp.bfloat16),
            pltpu.VMEM((2, rows, 2 * HALF), jnp.float32),
            pltpu.VMEM((2, 16, 2 * HALF), jnp.float32),
        ],
        compiler_params=pltpu.CompilerParams(vmem_limit_bytes=24 * 2**20),
        cost_estimate=pl.CostEstimate(
            flops=2 * PER * rows * width * 2 * HALF, bytes_accessed=3 * 2**20, transcendentals=0
        ),
        name="stack_group",
    )(sources, receivers, mask, basis, *earlier)


def order_kernel(place_ref, order_ref, *refs):
    mean_ref, weighted_ref = refs[-2:]
    middle, day = place_ref[0], place_ref[1]
    size = 2 * PER * 16

    def one(group):
        parts = [part[...].reshape(size, 2 * HALF) for part in group]
        full = jnp.dot(
            jnp.concatenate(parts, axis=0), order_ref[...], preferred_element_type=jnp.float32
        )
        for j in range(4):
            for k2 in range(PER):
                place = (0, (day ^ j) >> 1, middle ^ k2, (day ^ j) & 1)
                top = j * size + k2 * 16
                mean_ref[place] = full[top : top + 16, : 2 * MAXLAG + 1]
                top = top + PER * 16
                weighted_ref[place] = full[top : top + 16, : 2 * MAXLAG + 1]

    count = (len(refs) - 2) // 4
    for i in range(count):
        pl.when(pl.program_id(0) == i)(lambda i=i: one(refs[4 * i : 4 * i + 4]))


def order_groups(places, order, parts, outputs):
    whole = pl.BlockSpec(memory_space=pltpu.VMEM)
    count = len(parts) // 4
    shape = jax.ShapeDtypeStruct((4, 2, 4, 2, 16, 2 * MAXLAG + 1), jnp.float32)
    block = pl.BlockSpec(
        (1, 2, 4, 2, 16, 2 * MAXLAG + 1), lambda i, place: (place[2 + i], 0, 0, 0, 0, 0)
    )
    return pl.pallas_call(
        order_kernel,
        out_shape=(shape, shape),
        grid_spec=pltpu.PrefetchScalarGridSpec(
            num_scalar_prefetch=1,
            grid=(count,),
            in_specs=[whole] * (1 + len(parts)) + [pl.BlockSpec(memory_space=pl.ANY)] * len(outputs),
            out_specs=(block, block),
        ),
        input_output_aliases={2 + len(parts) + i: i for i in range(len(outputs))},
        compiler_params=pltpu.CompilerParams(vmem_limit_bytes=24 * 2**20),
        cost_estimate=pl.CostEstimate(flops=2**28, bytes_accessed=2**26, transcendentals=0),
        name="order_groups",
    )(places, order, *parts, *outputs)


def day_swap(x, k):
    return lax.ppermute(x, "day", [(i, i ^ k) for i in range(DAYS)])


def tile_swap(x, k):
    return lax.ppermute(x, "tile", [(i, i ^ k) for i in range(TILES)])


def turn(x, k):
    pairs = []
    for t in range(TILES):
        for xl in range(2):
            for core in range(2):
                to = (t & ~9) | ((xl ^ k) << 3) | core
                pairs.append((t * DAYS + 2 * xl + core, to * DAYS + 2 * ((t >> 3) & 1) + (t & 1)))
    return lax.ppermute(x, ("tile", "day"), pairs)


def on_device(source_spectra, receiver_spectra, valid_pairs):
    width = source_spectra.shape[3]
    tile, day = lax.axis_index("tile"), lax.axis_index("day")
    y, middle = tile >> 4, (tile >> 1) & 3
    shift = (((tile >> 3) & 1) * 2 + (tile & 1)) ^ day
    where = jnp.stack([y, middle, day, shift]).astype(jnp.int32)

    rec0 = jnp.transpose(receiver_spectra, (0, 2, 1, 3)).reshape(32 * PER, width)
    m0 = valid_pairs.reshape(PER, width).astype(jnp.bfloat16)
    rec0 = jnp.concatenate([rec0, jnp.pad(m0, ((0, 16 - PER), (0, 0)))], axis=0)
    rec2 = day_swap(rec0, 2)
    rec1 = day_swap(rec0, 1)
    rec3 = day_swap(rec2, 1)

    own = source_spectra.reshape(2 * PER, width)
    line = jnp.concatenate([own] + [tile_swap(own, 2 * k) for k in (1, 2, 3)], axis=0)
    pair = jnp.concatenate([line, day_swap(line, 1)], axis=0)
    second = jnp.concatenate([turn(pair, k) for k in range(2)], axis=0)
    groups = [second] + [tile_swap(second, 16 * k) for k in (1, 2, 3)]

    basis, order = half_basis(width), lag_order()
    receivers, masks = widen_receivers(where, (rec0, rec1, rec2, rec3))
    parts, earlier = {}, ()
    for k3 in (0, 1, 3, 2):
        mine = stack_group(groups[k3], receivers, masks[k3], basis, earlier)
        other = day_swap(mine, 2)
        far = day_swap(mine, 3) if k3 == 2 else day_swap(other, 1)
        parts[k3] = [mine, day_swap(mine, 1), other, far]
        earlier = (parts[0][0],)
    outputs = ()
    for k3 in (0, 1, 3, 2):
        places = jnp.stack([middle, day, y ^ k3]).astype(jnp.int32)
        outputs = order_groups(places, order, parts[k3], tuple(outputs))
    return tuple(out.reshape(TILES, 16, 2 * MAXLAG + 1) for out in outputs)


def solution(mesh):
    in_specs = (P("day", "tile", None, None), P("day", "tile", None, None), P("day", None, "tile"))
    out_specs = (P(None, "tile", None), P(None, "tile", None))
    return jax.shard_map(
        on_device, mesh=mesh, in_specs=in_specs, out_specs=out_specs, check_vma=False
    )
```

```python
import functools
import math

import jax
import jax.numpy as jnp
import numpy as np
from jax import lax
from jax.experimental import pallas as pl
from jax.experimental.pallas import tpu as pltpu
from jax.sharding import PartitionSpec as P

MAXLAG = 200
HALF = 256
TILES, DAYS = 64, 4

PER = 4


def fold_basis(frequency_count):
    samples, half, lanes = 2 * frequency_count, frequency_count // 2, HALF // 2
    even, odd = np.arange(0, MAXLAG + 1, 2)[None, :], np.arange(1, MAXLAG + 1, 2)[None, :]
    freq = np.arange(half)[:, None]
    tables = np.zeros((2, half, HALF))

    def angles(f, lag):
        return ((f * lag) % samples) * (2.0 * math.pi / samples)

    tables[0, :, : even.size] = np.cos(angles(freq, even))
    tables[0, :, lanes : lanes + odd.size] = np.sin(angles(freq, odd))
    tables[1, :, : odd.size] = np.cos(angles(freq, odd))
    tables[1, :, lanes : lanes + even.size] = np.sin(angles(freq, even))
    tables[0, 0, : even.size] = np.cos(angles(half, even))[0]
    tables[0, 0, lanes : lanes + odd.size] = np.sin(angles(half, odd))[0]
    tables[1, 0, : odd.size] = 0.5
    tables[1, 0, lanes - 1] = 0.5
    return jnp.asarray(tables * frequency_count ** (-0.5), jnp.bfloat16)


def reversal(half):
    table = np.zeros((half, half))
    table[0, 0] = 1.0
    table[np.arange(half - 1, 0, -1), np.arange(1, half)] = 1.0
    return jnp.asarray(table, jnp.bfloat16)


def lag_order():
    table = np.zeros((2 * HALF, 2 * HALF))
    lag = np.arange(MAXLAG + 1)
    lane = lag % 2 * (HALF // 2) + lag // 2
    table[lane, MAXLAG + lag] = 1.0
    table[HALF + lane[1:], MAXLAG - lag[1:]] = 1.0
    return jnp.asarray(table, jnp.bfloat16)


def fold_order(x, flip):
    half = x.shape[-1] // 2
    upper = jnp.dot(x[:, half:], flip, preferred_element_type=jnp.float32)
    return x[:, :half].astype(jnp.float32), upper


def widen_kernel(where_ref, rec0, rec1, rec2, rec3, flip_ref, out_ref, mask_ref, rows_ref):
    y, middle, day, shift = (where_ref[i] for i in range(4))
    width = out_ref.shape[-1]
    size, half = 32 * PER, width // 2
    for j, rec in enumerate((rec0, rec1, rec2, rec3)):
        k = j ^ shift
        lower, upper = fold_order(rec[:size], flip_ref[...])
        out_ref[pl.ds(k * PER, PER), :, :, :half] = lower.reshape(PER, 2, 16, half)
        out_ref[pl.ds(k * PER, PER), :, :, half:] = upper.reshape(PER, 2, 16, half)
        rows_ref[k] = rec[size:]
    rows = rows_ref[...].reshape(64, width)
    gap = lax.broadcasted_iota(jnp.int32, (16, width), 1) - lax.broadcasted_iota(jnp.int32, (16, width), 0)
    for k3 in range(4):
        picks = []
        for k2 in range(PER):
            source = source_index(y ^ k3, day, middle ^ k2)
            picks.append(jnp.where(gap == source * 16, 1.0, 0.0).astype(jnp.bfloat16))
        chosen = lax.dot_general(
            jnp.concatenate(picks, axis=0), rows, (((1,), (1,)), ((), ())),
            preferred_element_type=jnp.float32,
        )
        mask_ref[k3, :, :, :64] = chosen.reshape(PER, 16, 64)


def source_index(y, day, middle):
    return (y << 4) | ((day >> 1) << 3) | (middle << 1) | (day & 1)


def widen_receivers(where, receivers, flip):
    whole = pl.BlockSpec(memory_space=pltpu.VMEM)
    width = receivers[0].shape[-1]
    return pl.pallas_call(
        widen_kernel,
        out_shape=(
            jax.ShapeDtypeStruct((4 * PER, 2, 16, width), jnp.float32),
            jax.ShapeDtypeStruct((4, PER, 16, 128), jnp.float32),
        ),
        in_specs=[pl.BlockSpec(memory_space=pltpu.SMEM)] + [whole] * 5,
        out_specs=(whole, whole),
        scratch_shapes=[pltpu.VMEM((4, 16, width), jnp.bfloat16)],
        compiler_params=pltpu.CompilerParams(vmem_limit_bytes=16 * 2**20),
        name="widen_receivers",
    )(where, *receivers, flip)


def stack_kernel(src_ref, rec_ref, mask_ref, basis_ref, flip_ref, *refs):
    out_ref, src_f32, lhs, res, done = refs[-5:]
    days = 4 * PER
    size, half = days * 16, basis_ref.shape[1]
    lower, upper = fold_order(src_ref[...], flip_ref[...])
    src_f32[:, :half] = lower
    src_f32[:, half:] = upper
    alone = lax.broadcasted_iota(jnp.int32, (16, 256), 1) == 0
    for s in range(PER):
        p = s % 2
        for d in range(days):
            row = (d // PER * PER + s) * 2 * PER + d % PER * 2
            for lane in range(0, half, 256):
                pair = []
                for start in (lane, half + lane):
                    cols = slice(start, start + 256)
                    a = src_f32[row : row + 1, cols]
                    b = src_f32[row + 1 : row + 2, cols]
                    c = rec_ref[d, 0, :, cols]
                    e = rec_ref[d, 1, :, cols]
                    pair.append((a * c + b * e, a * e - b * c))
                cols = slice(lane, lane + 256)
                for i, (f, g) in enumerate(zip(*pair)):
                    plus, minus = f + g, f - g
                    if lane == 0:
                        plus, minus = jnp.where(alone, g, plus), jnp.where(alone, f, minus)
                    rows = slice(i * size + d * 16, i * size + d * 16 + 16)
                    lhs[p, 0, rows, cols] = plus.astype(jnp.bfloat16)
                    lhs[p, 1, rows, cols] = minus.astype(jnp.bfloat16)
        for i in range(2):
            res[p, i] = jnp.dot(lhs[p, i], basis_ref[i], preferred_element_type=jnp.float32)
        for h in range(0, 16, 8):
            zero = jnp.zeros((8, 128), jnp.float32)
            sums = [[zero] * 6 for _ in range(2)]
            count = zero
            for d in range(days):
                rows = slice(d * 16 + h, d * 16 + h + 8)
                low = slice(size + d * 16 + h, size + d * 16 + h + 8)
                col = (d // PER) * 16 + d % PER
                m = jnp.broadcast_to(mask_ref[s, h : h + 8, col : col + 1], (8, 128))
                count = count + m
                for i in range(2):
                    cos, sin = slice(0, 128), slice(128, 256)
                    rc, rs = res[p, i, rows, cos], res[p, 1 - i, rows, sin]
                    ic, is_ = res[p, i, low, cos], res[p, 1 - i, low, sin]
                    if i == 0:
                        rc = rc + res[p, 1, rows, 127:128]
                        ic = ic + res[p, 1, low, 127:128]
                    for sign, (u, v) in enumerate(((rc - is_, ic + rs), (rc + is_, ic - rs))):
                        w = m * lax.rsqrt(u * u + v * v + 0.0625)
                        acc = sums[i]
                        acc[3 * sign] = acc[3 * sign] + m * u
                        acc[3 * sign + 1] = acc[3 * sign + 1] + w * u
                        acc[3 * sign + 2] = acc[3 * sign + 2] + w * v
            inverse = 1.0 / jnp.maximum(count, 1.0)
            for i in range(2):
                for sign in range(2):
                    linear, real, imag = sums[i][3 * sign : 3 * sign + 3]
                    mean = linear * inverse
                    cols = slice(sign * HALF + i * 128, sign * HALF + i * 128 + 128)
                    done[0, h : h + 8, cols] = mean
                    done[1, h : h + 8, cols] = mean * ((real * real + imag * imag) * (inverse * inverse))
        out_ref[0, 0, s] = done[0].astype(jnp.bfloat16)
        out_ref[0, 1, s] = done[1].astype(jnp.bfloat16)


def stack_group(sources, receivers, mask, basis, flip, earlier):
    width = sources.shape[-1]
    whole = pl.BlockSpec(memory_space=pltpu.VMEM)
    rows = 2 * 4 * PER * 16
    return pl.pallas_call(
        stack_kernel,
        out_shape=jax.ShapeDtypeStruct((1, 2, PER, 16, 2 * HALF), jnp.bfloat16),
        in_specs=[whole] * 5 + [pl.BlockSpec(memory_space=pl.ANY)] * len(earlier),
        out_specs=whole,
        scratch_shapes=[
            pltpu.VMEM(sources.shape, jnp.float32),
            pltpu.VMEM((2, 2, rows, width // 2), jnp.bfloat16),
            pltpu.VMEM((2, 2, rows, HALF), jnp.float32),
            pltpu.VMEM((2, 16, 2 * HALF), jnp.float32),
        ],
        compiler_params=pltpu.CompilerParams(vmem_limit_bytes=24 * 2**20),
        cost_estimate=pl.CostEstimate(
            flops=2 * PER * rows * width * 2 * HALF, bytes_accessed=3 * 2**20, transcendentals=0
        ),
        name="stack_group",
    )(sources, receivers, mask, basis, flip, *earlier)


def order_kernel(count, place_ref, order_ref, *refs):
    parts = refs[:count]
    mean_ref, weighted_ref = refs[-2:]
    middle, day = place_ref[0], place_ref[1]
    size = 2 * PER * 16

    if parts[0].shape[0] == 2:
        parts = [ref.at[i : i + 1] for i in range(2) for ref in parts]
    full = jnp.dot(
        jnp.concatenate([part[...].reshape(size, 2 * HALF) for part in parts], axis=0),
        order_ref[...],
        preferred_element_type=jnp.float32,
    )
    for j in range(4):
        for k2 in range(PER):
            place = (0, (day ^ j) >> 1, middle ^ k2, (day ^ j) & 1)
            top = j * size + k2 * 16
            mean_ref[place] = full[top : top + 16, : 2 * MAXLAG + 1]
            top = top + PER * 16
            weighted_ref[place] = full[top : top + 16, : 2 * MAXLAG + 1]


def order_groups(places, order, parts, outputs):
    whole = pl.BlockSpec(memory_space=pltpu.VMEM)
    shape = jax.ShapeDtypeStruct((4, 2, 4, 2, 16, 2 * MAXLAG + 1), jnp.float32)
    block = pl.BlockSpec(
        (1, 2, 4, 2, 16, 2 * MAXLAG + 1), lambda i, place: (place[2 + i], 0, 0, 0, 0, 0)
    )
    return pl.pallas_call(
        functools.partial(order_kernel, len(parts)),
        out_shape=(shape, shape),
        grid_spec=pltpu.PrefetchScalarGridSpec(
            num_scalar_prefetch=1,
            grid=(1,),
            in_specs=[whole] * (1 + len(parts)) + [pl.BlockSpec(memory_space=pl.ANY)] * len(outputs),
            out_specs=(block, block),
        ),
        input_output_aliases={2 + len(parts) + i: i for i in range(len(outputs))},
        compiler_params=pltpu.CompilerParams(vmem_limit_bytes=24 * 2**20),
        cost_estimate=pl.CostEstimate(flops=2**28, bytes_accessed=2**26, transcendentals=0),
        name="order_groups",
    )(places, order, *parts, *outputs)


def day_swap(x, k):
    return lax.ppermute(x, "day", [(i, i ^ k) for i in range(DAYS)])


def tile_swap(x, k):
    return lax.ppermute(x, "tile", [(i, i ^ k) for i in range(TILES)])


def turn(x, k):
    pairs = []
    for t in range(TILES):
        for xl in range(2):
            for core in range(2):
                to = (t & ~9) | ((xl ^ k) << 3) | core
                pairs.append((t * DAYS + 2 * xl + core, to * DAYS + 2 * ((t >> 3) & 1) + (t & 1)))
    return lax.ppermute(x, ("tile", "day"), pairs)


def on_device(source_spectra, receiver_spectra, valid_pairs):
    width = source_spectra.shape[3]
    tile, day = lax.axis_index("tile"), lax.axis_index("day")
    y, middle = tile >> 4, (tile >> 1) & 3
    shift = (((tile >> 3) & 1) * 2 + (tile & 1)) ^ day
    where = jnp.stack([y, middle, day, shift]).astype(jnp.int32)

    rec0 = jnp.transpose(receiver_spectra, (0, 2, 1, 3)).reshape(32 * PER, width)
    m0 = valid_pairs.reshape(PER, width).astype(jnp.bfloat16)
    rec0 = jnp.concatenate([rec0, jnp.pad(m0, ((0, 16 - PER), (0, 0)))], axis=0)
    rec2 = day_swap(rec0, 2)
    rec1 = day_swap(rec0, 1)
    rec3 = day_swap(rec2, 1)

    own = source_spectra.reshape(2 * PER, width)
    line = jnp.concatenate([own] + [tile_swap(own, 2 * k) for k in (1, 2, 3)], axis=0)
    pair = jnp.concatenate([line, day_swap(line, 1)], axis=0)
    second = jnp.concatenate([turn(pair, k) for k in range(2)], axis=0)
    groups = [second] + [tile_swap(second, 16 * k) for k in (1, 2, 3)]

    basis, flip, order = fold_basis(width), reversal(width // 2), lag_order()
    receivers, masks = widen_receivers(where, (rec0, rec1, rec2, rec3), flip)
    parts, earlier = {}, ()
    for k3 in (0, 1, 3, 2):
        mine = stack_group(groups[k3], receivers, masks[k3], basis, flip, earlier)
        other = day_swap(mine, 2)
        if k3 == 2:
            parts[k3] = [mine, day_swap(mine, 1), other, day_swap(mine, 3)]
        else:
            near = jnp.concatenate([mine, other], axis=0)
            parts[k3] = [near, day_swap(near, 1)]
        earlier = earlier or (mine,)
    outputs = ()
    for k3 in (0, 1, 3, 2):
        places = jnp.stack([middle, day, y ^ k3]).astype(jnp.int32)
        outputs = order_groups(places, order, parts[k3], tuple(outputs))
    return tuple(out.reshape(TILES, 16, 2 * MAXLAG + 1) for out in outputs)


def solution(mesh):
    in_specs = (P("day", "tile", None, None), P("day", "tile", None, None), P("day", None, "tile"))
    out_specs = (P(None, "tile", None), P(None, "tile", None))
    return jax.shard_map(
        on_device, mesh=mesh, in_specs=in_specs, out_specs=out_specs, check_vma=False
    )
```

```python
import functools
import math

import jax
import jax.numpy as jnp
import numpy as np
from jax import lax
from jax.experimental import pallas as pl
from jax.experimental.pallas import tpu as pltpu
from jax.sharding import PartitionSpec as P

MAXLAG = 200
HALF = 256
TILES, DAYS = 64, 4

PER = 4


def fold_basis(frequency_count):
    samples, half, lanes = 2 * frequency_count, frequency_count // 2, HALF // 2
    even, odd = np.arange(0, MAXLAG + 1, 2)[None, :], np.arange(1, MAXLAG + 1, 2)[None, :]
    freq = np.arange(half)[:, None]
    tables = np.zeros((2, half, HALF))

    def angles(f, lag):
        return ((f * lag) % samples) * (2.0 * math.pi / samples)

    tables[0, :, : even.size] = np.cos(angles(freq, even))
    tables[0, :, lanes : lanes + odd.size] = np.sin(angles(freq, odd))
    tables[1, :, : odd.size] = np.cos(angles(freq, odd))
    tables[1, :, lanes : lanes + even.size] = np.sin(angles(freq, even))
    tables[0, 0, : even.size] = np.cos(angles(half, even))[0]
    tables[0, 0, lanes : lanes + odd.size] = np.sin(angles(half, odd))[0]
    tables[1, 0, : odd.size] = 0.5
    tables[1, 0, lanes - 1] = 0.5
    return jnp.asarray(tables * frequency_count ** (-0.5), jnp.bfloat16)


def reversal(half):
    table = np.zeros((half, half))
    table[0, 0] = 1.0
    table[np.arange(half - 1, 0, -1), np.arange(1, half)] = 1.0
    return jnp.asarray(table, jnp.bfloat16)


def lag_order():
    table = np.zeros((2 * HALF, 2 * HALF))
    lag = np.arange(MAXLAG + 1)
    lane = lag % 2 * (HALF // 2) + lag // 2
    table[lane, MAXLAG + lag] = 1.0
    table[HALF + lane[1:], MAXLAG - lag[1:]] = 1.0
    return jnp.asarray(table, jnp.bfloat16)


def fold_order(x, flip):
    half = x.shape[-1] // 2
    upper = jnp.dot(x[:, half:], flip, preferred_element_type=jnp.float32)
    return x[:, :half].astype(jnp.float32), upper


def widen_kernel(where_ref, rec0, rec1, rec2, rec3, flip_ref, out_ref, mask_ref, rows_ref):
    y, middle, day, shift = (where_ref[i] for i in range(4))
    width = out_ref.shape[-1]
    size, half = 32 * PER, width // 2
    for j, rec in enumerate((rec0, rec1, rec2, rec3)):
        k = j ^ shift
        lower, upper = fold_order(rec[:size], flip_ref[...])
        out_ref[pl.ds(k * PER, PER), :, :, :half] = lower.reshape(PER, 2, 16, half)
        out_ref[pl.ds(k * PER, PER), :, :, half:] = upper.reshape(PER, 2, 16, half)
        rows_ref[k] = rec[size:]
    rows = rows_ref[...].reshape(64, width)
    gap = lax.broadcasted_iota(jnp.int32, (16, width), 1) - lax.broadcasted_iota(jnp.int32, (16, width), 0)
    for k3 in range(4):
        picks = []
        for k2 in range(PER):
            source = source_index(y ^ k3, day, middle ^ k2)
            picks.append(jnp.where(gap == source * 16, 1.0, 0.0).astype(jnp.bfloat16))
        chosen = lax.dot_general(
            jnp.concatenate(picks, axis=0), rows, (((1,), (1,)), ((), ())),
            preferred_element_type=jnp.float32,
        )
        mask_ref[k3, :, :, :64] = chosen.reshape(PER, 16, 64)


def source_index(y, day, middle):
    return (y << 4) | ((day >> 1) << 3) | (middle << 1) | (day & 1)


def widen_receivers(where, receivers, flip):
    whole = pl.BlockSpec(memory_space=pltpu.VMEM)
    width = receivers[0].shape[-1]
    return pl.pallas_call(
        widen_kernel,
        out_shape=(
            jax.ShapeDtypeStruct((4 * PER, 2, 16, width), jnp.float32),
            jax.ShapeDtypeStruct((4, PER, 16, 128), jnp.float32),
        ),
        in_specs=[pl.BlockSpec(memory_space=pltpu.SMEM)] + [whole] * 5,
        out_specs=(whole, whole),
        scratch_shapes=[pltpu.VMEM((4, 16, width), jnp.bfloat16)],
        compiler_params=pltpu.CompilerParams(vmem_limit_bytes=16 * 2**20),
        name="widen_receivers",
    )(where, *receivers, flip)


def stack_kernel(src_ref, rec_ref, mask_ref, basis_ref, flip_ref, *refs):
    out_ref, src_f32, lhs, res, done = refs[-5:]
    days = 4 * PER
    size, half = days * 16, basis_ref.shape[1]
    lower, upper = fold_order(src_ref[...], flip_ref[...])
    src_f32[:, :half] = lower
    src_f32[:, half:] = upper
    alone = lax.broadcasted_iota(jnp.int32, (16, 256), 1) == 0
    for s in range(PER):
        p = s % 2
        for d in range(days):
            row = (d // PER * PER + s) * 2 * PER + d % PER * 2
            for lane in range(0, half, 256):
                pair = []
                for start in (lane, half + lane):
                    cols = slice(start, start + 256)
                    a = src_f32[row : row + 1, cols]
                    b = src_f32[row + 1 : row + 2, cols]
                    c = rec_ref[d, 0, :, cols]
                    e = rec_ref[d, 1, :, cols]
                    pair.append((a * c + b * e, a * e - b * c))
                cols = slice(lane, lane + 256)
                for i, (f, g) in enumerate(zip(*pair)):
                    f, g = f.astype(jnp.bfloat16), g.astype(jnp.bfloat16)
                    plus, minus = f + g, f - g
                    if lane == 0:
                        plus, minus = jnp.where(alone, g, plus), jnp.where(alone, f, minus)
                    rows = slice(i * size + d * 16, i * size + d * 16 + 16)
                    lhs[p, 0, rows, cols] = plus
                    lhs[p, 1, rows, cols] = minus
        for i in range(2):
            res[p, i] = jnp.dot(lhs[p, i], basis_ref[i], preferred_element_type=jnp.float32)
        for h in range(0, 16, 8):
            zero = jnp.zeros((8, 128), jnp.float32)
            sums = [[zero] * 6 for _ in range(2)]
            count = zero
            for d in range(days):
                rows = slice(d * 16 + h, d * 16 + h + 8)
                low = slice(size + d * 16 + h, size + d * 16 + h + 8)
                col = (d // PER) * 16 + d % PER
                m = jnp.broadcast_to(mask_ref[s, h : h + 8, col : col + 1], (8, 128))
                count = count + m
                for i in range(2):
                    cos, sin = slice(0, 128), slice(128, 256)
                    rc, rs = res[p, i, rows, cos], res[p, 1 - i, rows, sin]
                    ic, is_ = res[p, i, low, cos], res[p, 1 - i, low, sin]
                    if i == 0:
                        rc = rc + res[p, 1, rows, 127:128]
                        ic = ic + res[p, 1, low, 127:128]
                    for sign, (u, v) in enumerate(((rc - is_, ic + rs), (rc + is_, ic - rs))):
                        w = m * lax.rsqrt(u * u + v * v + 0.0625)
                        acc = sums[i]
                        acc[3 * sign] = acc[3 * sign] + m * u
                        acc[3 * sign + 1] = acc[3 * sign + 1] + w * u
                        acc[3 * sign + 2] = acc[3 * sign + 2] + w * v
            inverse = 1.0 / jnp.maximum(count, 1.0)
            for i in range(2):
                for sign in range(2):
                    linear, real, imag = sums[i][3 * sign : 3 * sign + 3]
                    mean = linear * inverse
                    cols = slice(sign * HALF + i * 128, sign * HALF + i * 128 + 128)
                    done[0, h : h + 8, cols] = mean
                    done[1, h : h + 8, cols] = mean * ((real * real + imag * imag) * (inverse * inverse))
        out_ref[0, 0, s] = done[0].astype(jnp.bfloat16)
        out_ref[0, 1, s] = done[1].astype(jnp.bfloat16)


def stack_group(sources, receivers, mask, basis, flip, earlier):
    width = sources.shape[-1]
    whole = pl.BlockSpec(memory_space=pltpu.VMEM)
    rows = 2 * 4 * PER * 16
    return pl.pallas_call(
        stack_kernel,
        out_shape=jax.ShapeDtypeStruct((1, 2, PER, 16, 2 * HALF), jnp.bfloat16),
        in_specs=[whole] * 5 + [pl.BlockSpec(memory_space=pl.ANY)] * len(earlier),
        out_specs=whole,
        scratch_shapes=[
            pltpu.VMEM(sources.shape, jnp.float32),
            pltpu.VMEM((2, 2, rows, width // 2), jnp.bfloat16),
            pltpu.VMEM((2, 2, rows, HALF), jnp.float32),
            pltpu.VMEM((2, 16, 2 * HALF), jnp.float32),
        ],
        compiler_params=pltpu.CompilerParams(vmem_limit_bytes=24 * 2**20),
        cost_estimate=pl.CostEstimate(
            flops=2 * PER * rows * width * 2 * HALF, bytes_accessed=3 * 2**20, transcendentals=0
        ),
        name="stack_group",
    )(sources, receivers, mask, basis, flip, *earlier)


def order_kernel(count, place_ref, order_ref, *refs):
    parts = refs[:count]
    mean_ref, weighted_ref = refs[-2:]
    middle, day = place_ref[0], place_ref[1]
    size = 2 * PER * 16

    if parts[0].shape[0] == 2:
        parts = [ref.at[i : i + 1] for i in range(2) for ref in parts]
    full = jnp.dot(
        jnp.concatenate([part[...].reshape(size, 2 * HALF) for part in parts], axis=0),
        order_ref[...],
        preferred_element_type=jnp.float32,
    )
    for j in range(4):
        for k2 in range(PER):
            place = (0, (day ^ j) >> 1, middle ^ k2, (day ^ j) & 1)
            top = j * size + k2 * 16
            mean_ref[place] = full[top : top + 16, : 2 * MAXLAG + 1]
            top = top + PER * 16
            weighted_ref[place] = full[top : top + 16, : 2 * MAXLAG + 1]


def order_groups(places, order, parts, outputs):
    whole = pl.BlockSpec(memory_space=pltpu.VMEM)
    shape = jax.ShapeDtypeStruct((4, 2, 4, 2, 16, 2 * MAXLAG + 1), jnp.float32)
    block = pl.BlockSpec(
        (1, 2, 4, 2, 16, 2 * MAXLAG + 1), lambda i, place: (place[2 + i], 0, 0, 0, 0, 0)
    )
    return pl.pallas_call(
        functools.partial(order_kernel, len(parts)),
        out_shape=(shape, shape),
        grid_spec=pltpu.PrefetchScalarGridSpec(
            num_scalar_prefetch=1,
            grid=(1,),
            in_specs=[whole] * (1 + len(parts)) + [pl.BlockSpec(memory_space=pl.ANY)] * len(outputs),
            out_specs=(block, block),
        ),
        input_output_aliases={2 + len(parts) + i: i for i in range(len(outputs))},
        compiler_params=pltpu.CompilerParams(vmem_limit_bytes=24 * 2**20),
        cost_estimate=pl.CostEstimate(flops=2**28, bytes_accessed=2**26, transcendentals=0),
        name="order_groups",
    )(places, order, *parts, *outputs)


def day_swap(x, k):
    return lax.ppermute(x, "day", [(i, i ^ k) for i in range(DAYS)])


def tile_swap(x, k):
    return lax.ppermute(x, "tile", [(i, i ^ k) for i in range(TILES)])


def turn(x, k):
    pairs = []
    for t in range(TILES):
        for xl in range(2):
            for core in range(2):
                to = (t & ~9) | ((xl ^ k) << 3) | core
                pairs.append((t * DAYS + 2 * xl + core, to * DAYS + 2 * ((t >> 3) & 1) + (t & 1)))
    return lax.ppermute(x, ("tile", "day"), pairs)


def on_device(source_spectra, receiver_spectra, valid_pairs):
    width = source_spectra.shape[3]
    tile, day = lax.axis_index("tile"), lax.axis_index("day")
    y, middle = tile >> 4, (tile >> 1) & 3
    shift = (((tile >> 3) & 1) * 2 + (tile & 1)) ^ day
    where = jnp.stack([y, middle, day, shift]).astype(jnp.int32)

    rec0 = jnp.transpose(receiver_spectra, (0, 2, 1, 3)).reshape(32 * PER, width)
    m0 = valid_pairs.reshape(PER, width).astype(jnp.bfloat16)
    rec0 = jnp.concatenate([rec0, jnp.pad(m0, ((0, 16 - PER), (0, 0)))], axis=0)
    rec2 = day_swap(rec0, 2)
    rec1 = day_swap(rec0, 1)
    rec3 = day_swap(rec2, 1)

    own = source_spectra.reshape(2 * PER, width)
    line = jnp.concatenate([own] + [tile_swap(own, 2 * k) for k in (1, 2, 3)], axis=0)
    pair = jnp.concatenate([line, day_swap(line, 1)], axis=0)
    second = jnp.concatenate([turn(pair, k) for k in range(2)], axis=0)
    groups = [second] + [tile_swap(second, 16 * k) for k in (1, 2, 3)]

    basis, flip, order = fold_basis(width), reversal(width // 2), lag_order()
    receivers, masks = widen_receivers(where, (rec0, rec1, rec2, rec3), flip)
    parts, earlier = {}, ()
    for k3 in (0, 1, 3, 2):
        mine = stack_group(groups[k3], receivers, masks[k3], basis, flip, earlier)
        other = day_swap(mine, 2)
        if k3 == 2:
            parts[k3] = [mine, day_swap(mine, 1), other, day_swap(mine, 3)]
        else:
            near = jnp.concatenate([mine, other], axis=0)
            parts[k3] = [near, day_swap(near, 1)]
        earlier = earlier or (mine,)
    outputs = ()
    for k3 in (0, 1, 3, 2):
        places = jnp.stack([middle, day, y ^ k3]).astype(jnp.int32)
        outputs = order_groups(places, order, parts[k3], tuple(outputs))
    return tuple(out.reshape(TILES, 16, 2 * MAXLAG + 1) for out in outputs)


def solution(mesh):
    in_specs = (P("day", "tile", None, None), P("day", "tile", None, None), P("day", None, "tile"))
    out_specs = (P(None, "tile", None), P(None, "tile", None))
    return jax.shard_map(
        on_device, mesh=mesh, in_specs=in_specs, out_specs=out_specs, check_vma=False
    )
```

```python
import functools
import math

import jax
import jax.numpy as jnp
import numpy as np
from jax import lax
from jax.experimental import pallas as pl
from jax.experimental.pallas import tpu as pltpu
from jax.sharding import PartitionSpec as P

MAXLAG = 200
HALF = 256
TILES, DAYS = 64, 4

PER = 4


def fold_basis(frequency_count):
    samples, half, lanes = 2 * frequency_count, frequency_count // 2, HALF // 2
    even, odd = np.arange(0, MAXLAG + 1, 2)[None, :], np.arange(1, MAXLAG + 1, 2)[None, :]
    freq = np.arange(half)[:, None]
    tables = np.zeros((2, half, HALF))

    def angles(f, lag):
        return ((f * lag) % samples) * (2.0 * math.pi / samples)

    tables[0, :, : even.size] = np.cos(angles(freq, even))
    tables[0, :, lanes : lanes + odd.size] = np.sin(angles(freq, odd))
    tables[1, :, : odd.size] = np.cos(angles(freq, odd))
    tables[1, :, lanes : lanes + even.size] = np.sin(angles(freq, even))
    tables[0, 0, : even.size] = np.cos(angles(half, even))[0]
    tables[0, 0, lanes : lanes + odd.size] = np.sin(angles(half, odd))[0]
    tables[1, 0, : odd.size] = 0.5
    tables[1, 0, lanes - 1] = 0.5
    return jnp.asarray(tables * frequency_count ** (-0.5), jnp.bfloat16)


def reversal(half):
    table = np.zeros((half, half))
    table[0, 0] = 1.0
    table[np.arange(half - 1, 0, -1), np.arange(1, half)] = 1.0
    return jnp.asarray(table, jnp.bfloat16)


def lag_order():
    table = np.zeros((2 * HALF, 2 * HALF))
    lag = np.arange(MAXLAG + 1)
    lane = lag % 2 * (HALF // 2) + lag // 2
    table[lane, MAXLAG + lag] = 1.0
    table[HALF + lane[1:], MAXLAG - lag[1:]] = 1.0
    return jnp.asarray(table, jnp.bfloat16)


def fold_order(x, flip):
    half = x.shape[-1] // 2
    upper = jnp.dot(x[:, half:], flip, preferred_element_type=jnp.float32)
    return x[:, :half].astype(jnp.float32), upper


def widen_kernel(where_ref, rec0, rec1, rec2, rec3, flip_ref, out_ref, mask_ref, rows_ref):
    y, middle, day, shift = (where_ref[i] for i in range(4))
    width = out_ref.shape[-1]
    size, half = 32 * PER, width // 2
    for j, rec in enumerate((rec0, rec1, rec2, rec3)):
        k = j ^ shift
        lower, upper = fold_order(rec[:size], flip_ref[...])
        out_ref[pl.ds(k * PER, PER), :, :, :half] = lower.reshape(PER, 2, 16, half)
        out_ref[pl.ds(k * PER, PER), :, :, half:] = upper.reshape(PER, 2, 16, half)
        rows_ref[k] = rec[size:]
    rows = rows_ref[...].reshape(64, width)
    gap = lax.broadcasted_iota(jnp.int32, (16, width), 1) - lax.broadcasted_iota(jnp.int32, (16, width), 0)
    for k3 in range(4):
        picks = []
        for k2 in range(PER):
            source = source_index(y ^ k3, day, middle ^ k2)
            picks.append(jnp.where(gap == source * 16, 1.0, 0.0).astype(jnp.bfloat16))
        chosen = lax.dot_general(
            jnp.concatenate(picks, axis=0), rows, (((1,), (1,)), ((), ())),
            preferred_element_type=jnp.float32,
        )
        mask_ref[k3, :, :, :64] = chosen.reshape(PER, 16, 64)


def source_index(y, day, middle):
    return (y << 4) | ((day >> 1) << 3) | (middle << 1) | (day & 1)


def widen_receivers(where, receivers, flip):
    whole = pl.BlockSpec(memory_space=pltpu.VMEM)
    width = receivers[0].shape[-1]
    return pl.pallas_call(
        widen_kernel,
        out_shape=(
            jax.ShapeDtypeStruct((4 * PER, 2, 16, width), jnp.float32),
            jax.ShapeDtypeStruct((4, PER, 16, 128), jnp.float32),
        ),
        in_specs=[pl.BlockSpec(memory_space=pltpu.SMEM)] + [whole] * 5,
        out_specs=(whole, whole),
        scratch_shapes=[pltpu.VMEM((4, 16, width), jnp.bfloat16)],
        compiler_params=pltpu.CompilerParams(vmem_limit_bytes=16 * 2**20),
        name="widen_receivers",
    )(where, *receivers, flip)


def stack_kernel(src_ref, rec_ref, mask_ref, basis_ref, flip_ref, *refs):
    out_ref, src_f32, lhs, res, done = refs[-5:]
    days = 4 * PER
    size, half = days * 16, basis_ref.shape[1]
    lower, upper = fold_order(src_ref[...], flip_ref[...])
    src_f32[:, :half] = lower
    src_f32[:, half:] = upper
    alone = lax.broadcasted_iota(jnp.int32, (16, 512), 1) == 0
    for s in range(PER):
        p = s % 2
        for d in range(days):
            row = (d // PER * PER + s) * 2 * PER + d % PER * 2
            for lane in range(0, half, 512):
                pair = []
                for start in (lane, half + lane):
                    cols = slice(start, start + 512)
                    a = src_f32[row : row + 1, cols]
                    b = src_f32[row + 1 : row + 2, cols]
                    c = rec_ref[d, 0, :, cols]
                    e = rec_ref[d, 1, :, cols]
                    pair.append((a * c + b * e, a * e - b * c))
                cols = slice(lane, lane + 512)
                for i, (f, g) in enumerate(zip(*pair)):
                    f, g = f.astype(jnp.bfloat16), g.astype(jnp.bfloat16)
                    plus, minus = f + g, f - g
                    if lane == 0:
                        plus, minus = jnp.where(alone, g, plus), jnp.where(alone, f, minus)
                    rows = slice(i * size + d * 16, i * size + d * 16 + 16)
                    lhs[p, 0, rows, cols] = plus
                    lhs[p, 1, rows, cols] = minus
        for i in range(2):
            res[p, i] = jnp.dot(lhs[p, i], basis_ref[i], preferred_element_type=jnp.float32)
        for h in range(0, 16, 8):
            zero = jnp.zeros((8, 128), jnp.float32)
            sums = [[zero] * 6 for _ in range(2)]
            count = zero
            for d in range(days):
                rows = slice(d * 16 + h, d * 16 + h + 8)
                low = slice(size + d * 16 + h, size + d * 16 + h + 8)
                col = (d // PER) * 16 + d % PER
                m = jnp.broadcast_to(mask_ref[s, h : h + 8, col : col + 1], (8, 128))
                count = count + m
                for i in range(2):
                    cos, sin = slice(0, 128), slice(128, 256)
                    rc, rs = res[p, i, rows, cos], res[p, 1 - i, rows, sin]
                    ic, is_ = res[p, i, low, cos], res[p, 1 - i, low, sin]
                    if i == 0:
                        rc = rc + res[p, 1, rows, 127:128]
                        ic = ic + res[p, 1, low, 127:128]
                    for sign, (u, v) in enumerate(((rc - is_, ic + rs), (rc + is_, ic - rs))):
                        w = m * lax.rsqrt(u * u + v * v + 0.0625)
                        acc = sums[i]
                        acc[3 * sign] = acc[3 * sign] + m * u
                        acc[3 * sign + 1] = acc[3 * sign + 1] + w * u
                        acc[3 * sign + 2] = acc[3 * sign + 2] + w * v
            inverse = 1.0 / jnp.maximum(count, 1.0)
            for i in range(2):
                for sign in range(2):
                    linear, real, imag = sums[i][3 * sign : 3 * sign + 3]
                    mean = linear * inverse
                    cols = slice(sign * HALF + i * 128, sign * HALF + i * 128 + 128)
                    done[0, h : h + 8, cols] = mean
                    done[1, h : h + 8, cols] = mean * ((real * real + imag * imag) * (inverse * inverse))
        out_ref[0, 0, s] = done[0].astype(jnp.bfloat16)
        out_ref[0, 1, s] = done[1].astype(jnp.bfloat16)


def stack_group(sources, receivers, mask, basis, flip, earlier):
    width = sources.shape[-1]
    whole = pl.BlockSpec(memory_space=pltpu.VMEM)
    rows = 2 * 4 * PER * 16
    return pl.pallas_call(
        stack_kernel,
        out_shape=jax.ShapeDtypeStruct((1, 2, PER, 16, 2 * HALF), jnp.bfloat16),
        in_specs=[whole] * 5 + [pl.BlockSpec(memory_space=pl.ANY)] * len(earlier),
        out_specs=whole,
        scratch_shapes=[
            pltpu.VMEM(sources.shape, jnp.float32),
            pltpu.VMEM((2, 2, rows, width // 2), jnp.bfloat16),
            pltpu.VMEM((2, 2, rows, HALF), jnp.float32),
            pltpu.VMEM((2, 16, 2 * HALF), jnp.float32),
        ],
        compiler_params=pltpu.CompilerParams(vmem_limit_bytes=24 * 2**20),
        cost_estimate=pl.CostEstimate(
            flops=2 * PER * rows * width * 2 * HALF, bytes_accessed=3 * 2**20, transcendentals=0
        ),
        name="stack_group",
    )(sources, receivers, mask, basis, flip, *earlier)


def order_kernel(count, place_ref, order_ref, *refs):
    parts = refs[:count]
    mean_ref, weighted_ref = refs[-2:]
    middle, day = place_ref[0], place_ref[1]
    size = 2 * PER * 16

    if parts[0].shape[0] == 2:
        parts = [ref.at[i : i + 1] for i in range(2) for ref in parts]
    full = jnp.dot(
        jnp.concatenate([part[...].reshape(size, 2 * HALF) for part in parts], axis=0),
        order_ref[...],
        preferred_element_type=jnp.float32,
    )
    for j in range(4):
        for k2 in range(PER):
            place = (0, (day ^ j) >> 1, middle ^ k2, (day ^ j) & 1)
            top = j * size + k2 * 16
            mean_ref[place] = full[top : top + 16, : 2 * MAXLAG + 1]
            top = top + PER * 16
            weighted_ref[place] = full[top : top + 16, : 2 * MAXLAG + 1]


def order_groups(places, order, parts, outputs):
    whole = pl.BlockSpec(memory_space=pltpu.VMEM)
    shape = jax.ShapeDtypeStruct((4, 2, 4, 2, 16, 2 * MAXLAG + 1), jnp.float32)
    block = pl.BlockSpec(
        (1, 2, 4, 2, 16, 2 * MAXLAG + 1), lambda i, place: (place[2 + i], 0, 0, 0, 0, 0)
    )
    return pl.pallas_call(
        functools.partial(order_kernel, len(parts)),
        out_shape=(shape, shape),
        grid_spec=pltpu.PrefetchScalarGridSpec(
            num_scalar_prefetch=1,
            grid=(1,),
            in_specs=[whole] * (1 + len(parts)) + [pl.BlockSpec(memory_space=pl.ANY)] * len(outputs),
            out_specs=(block, block),
        ),
        input_output_aliases={2 + len(parts) + i: i for i in range(len(outputs))},
        compiler_params=pltpu.CompilerParams(vmem_limit_bytes=24 * 2**20),
        cost_estimate=pl.CostEstimate(flops=2**28, bytes_accessed=2**26, transcendentals=0),
        name="order_groups",
    )(places, order, *parts, *outputs)


def day_swap(x, k):
    return lax.ppermute(x, "day", [(i, i ^ k) for i in range(DAYS)])


def tile_swap(x, k):
    return lax.ppermute(x, "tile", [(i, i ^ k) for i in range(TILES)])


def turn(x, k):
    pairs = []
    for t in range(TILES):
        for xl in range(2):
            for core in range(2):
                to = (t & ~9) | ((xl ^ k) << 3) | core
                pairs.append((t * DAYS + 2 * xl + core, to * DAYS + 2 * ((t >> 3) & 1) + (t & 1)))
    return lax.ppermute(x, ("tile", "day"), pairs)


def on_device(source_spectra, receiver_spectra, valid_pairs):
    width = source_spectra.shape[3]
    tile, day = lax.axis_index("tile"), lax.axis_index("day")
    y, middle = tile >> 4, (tile >> 1) & 3
    shift = (((tile >> 3) & 1) * 2 + (tile & 1)) ^ day
    where = jnp.stack([y, middle, day, shift]).astype(jnp.int32)

    rec0 = jnp.transpose(receiver_spectra, (0, 2, 1, 3)).reshape(32 * PER, width)
    m0 = valid_pairs.reshape(PER, width).astype(jnp.bfloat16)
    rec0 = jnp.concatenate([rec0, jnp.pad(m0, ((0, 16 - PER), (0, 0)))], axis=0)
    rec2 = day_swap(rec0, 2)
    rec1 = day_swap(rec0, 1)
    rec3 = day_swap(rec2, 1)

    own = source_spectra.reshape(2 * PER, width)
    line = jnp.concatenate([own] + [tile_swap(own, 2 * k) for k in (1, 2, 3)], axis=0)
    pair = jnp.concatenate([line, day_swap(line, 1)], axis=0)
    second = jnp.concatenate([turn(pair, k) for k in range(2)], axis=0)
    groups = [second] + [tile_swap(second, 16 * k) for k in (1, 2, 3)]

    basis, flip, order = fold_basis(width), reversal(width // 2), lag_order()
    receivers, masks = widen_receivers(where, (rec0, rec1, rec2, rec3), flip)
    parts, earlier = {}, ()
    for k3 in (0, 1, 3, 2):
        mine = stack_group(groups[k3], receivers, masks[k3], basis, flip, earlier)
        other = day_swap(mine, 2)
        if k3 == 2:
            parts[k3] = [mine, day_swap(mine, 1), other, day_swap(mine, 3)]
        else:
            near = jnp.concatenate([mine, other], axis=0)
            parts[k3] = [near, day_swap(near, 1)]
        earlier = earlier or (mine,)
    outputs = ()
    for k3 in (0, 1, 3, 2):
        places = jnp.stack([middle, day, y ^ k3]).astype(jnp.int32)
        outputs = order_groups(places, order, parts[k3], tuple(outputs))
    return tuple(out.reshape(TILES, 16, 2 * MAXLAG + 1) for out in outputs)


def solution(mesh):
    in_specs = (P("day", "tile", None, None), P("day", "tile", None, None), P("day", None, "tile"))
    out_specs = (P(None, "tile", None), P(None, "tile", None))
    return jax.shard_map(
        on_device, mesh=mesh, in_specs=in_specs, out_specs=out_specs, check_vma=False
    )
```
